512 devices in a mesh: col: 32 (over x, z_lo, core), row: 16 (over z_hi, y).
Axes of the slice: x: 4, y: 4, z: 16 (z_hi: 4, z_lo: 4; z = z_hi * 4 + z_lo), core: 2. Of those that a mesh axis runs over, the one named last changes fastest.
Arguments:
- features: bfloat16 [65536, 256], P(('col', 'row')), may hold values from -6 to 6
- grad_out: bfloat16 [65536, 256], P(('col', 'row')), may hold values from -6 to 6
- weight: bfloat16 [256, 256], replicated, may hold values from -4 to 4
- bias: float32 [256], replicated, may hold values from -3 to 3
- tile_rows: int32 [32, 16, 32], P('col', 'row'), may hold values from 0 to 15
- tile_cols: int32 [32, 16, 32], P('col', 'row'), may hold values from 0 to 31
- tile_weights: bfloat16 [32, 16, 32, 128, 128], P('col', 'row'), may hold values from 0 to 0.051, as said below
- tile_count: int32 [32, 16], P('col', 'row'), may hold values from 8 to 32, as said below
Outputs:
- node_out: bfloat16 [65536, 256], P(('col', 'row'))
- grad_features: bfloat16 [65536, 256], P(('col', 'row'))
- grad_weight: float32 [256, 256], replicated
- grad_bias: float32 [256], replicated
The draws below stay inside these ranges and needn't reach their ends.
Inputs may be any that keep to these rules, and one draw needn't show every extreme that they name: `tile_rows`: tile slots may repeat a position; their entries add up. `tile_weights`: nonnegative edge weights; most entries are zero. `tile_count`: some device uses all 32 slots.
All inputs are finite; a program needn't handle non-finite values.
Results may differ from the reference program's by a relative error of at most 0.017.
Values may be sent and summed in bfloat16 or wider, within the bound.
No kernel may reach another device: no remote copies, remote signals or barrier semaphores. Data moves between devices by JAX's collectives and lax.ppermute only.
A program may use at most 64 MiB of HBM per device.

```python
import math
import jax
import jax.numpy as jnp
from jax import lax

H = 256
TILE = 128
NODE_DEV = 128
TILES_DEV = 32
NODES = 65536
N_COL = 32
N_ROW = 16


def draw_tile_weights(key, part):
    key = jax.random.fold_in(key, 11)
    shape = (N_COL, N_ROW, TILES_DEV, TILE, TILE)
    uniform_draw = jax.random.uniform(key, shape, jnp.float32)
    present = uniform_draw < 0.0625
    ratio = jnp.clip(uniform_draw * 16.0, 0.0, 1.0)
    mass = 0.005 * jnp.exp(ratio * math.log(10.0))
    return jnp.where(present, mass, 0.0).astype(jnp.bfloat16)


def draw_tile_count(key, part):
    key = jax.random.fold_in(key, 23)
    count_key, pick_key = jax.random.split(key)
    lowest = max(1, TILES_DEV // 4)
    counts = jax.random.randint(count_key, (N_COL * N_ROW,), lowest, TILES_DEV + 1)
    chosen = jax.random.randint(pick_key, (), 0, N_COL * N_ROW)
    counts = counts.at[chosen].set(TILES_DEV)
    return counts.reshape(N_COL, N_ROW).astype(jnp.int32)


def place_ends(entries, own_key, least, top_value):
    longest = entries.shape.index(max(entries.shape))
    spots = []
    for shift in (0, 1):
        where = [jax.random.randint(jax.random.fold_in(own_key, axis), (), 0, length) for axis, length in enumerate(entries.shape)]
        where[longest] = (where[longest] + shift) % entries.shape[longest]
        spots.append(tuple(where))
    return entries.at[spots[0]].set(least).at[spots[1]].set(top_value)


def block_scale(stream_key, shape, cuts, smallest, top_value):
    def one(position, blocks):
        draws = jax.random.uniform(jax.random.fold_in(jax.random.fold_in(stream_key, 6), position), (blocks,), jnp.float32, smallest / len(cuts), top_value / len(cuts))
        return jnp.repeat(jnp.exp(draws), shape[position] // blocks).reshape((-1,) + (1,) * (len(shape) - position - 1))

    factor_of = one(*cuts[0])
    for cut in cuts[1:]:
        factor_of = factor_of * one(*cut)
    return factor_of


def noise(key, dims, deviation, reach, pieces=(), held_as=jnp.bfloat16):
    result = jax.random.normal(key, dims, jnp.float32) * deviation
    if len(pieces) > 0:
        result = block_scale(key, dims, pieces, -0.22, 0.18) * result
    return jnp.clip(result, min=-reach, max=reach).astype(held_as)


def setup_inputs(seed: int = 0) -> dict:
    streams_of = jax.random.split(jax.random.key(seed), 9)
    return {
        "features": noise(streams_of[0], (NODES, H), 1.0, 6.0, ((0, 512),)),
        "grad_out": noise(streams_of[1], (NODES, H), 1.0, 6.0, ((0, 512),)),
        "weight": noise(streams_of[2], (H, H), 0.8, 4.0),
        "bias": noise(streams_of[3], (H,), 0.5, 3.0, (), jnp.float32),
        "tile_rows": place_ends(jax.random.randint(streams_of[4], (N_COL, N_ROW, TILES_DEV), 0, N_ROW * NODE_DEV // TILE), jax.random.fold_in(streams_of[4], 1), 0, (N_ROW * NODE_DEV // TILE) - 1).astype(jnp.int32),
        "tile_cols": place_ends(jax.random.randint(streams_of[5], (N_COL, N_ROW, TILES_DEV), 0, N_COL * NODE_DEV // TILE), jax.random.fold_in(streams_of[5], 1), 0, (N_COL * NODE_DEV // TILE) - 1).astype(jnp.int32),
        "tile_weights": draw_tile_weights(jax.random.fold_in(streams_of[8], 71), 0),
        "tile_count": draw_tile_count(jax.random.fold_in(streams_of[8], 71), 0),
    }


def silu_slope(pre):
    sigmoid_val = jax.nn.sigmoid(pre)
    return sigmoid_val * (1.0 + pre * (1.0 - sigmoid_val))

def live_weights(tile_weights, tile_count, col_idx, row_idx):
    slot_ids = jnp.arange(TILES_DEV)
    live = (slot_ids < tile_count[col_idx, row_idx]).astype(jnp.float32)
    return tile_weights[col_idx, row_idx].astype(jnp.float32) * live[:, None, None]

def reference(features, grad_out, weight, bias, tile_rows, tile_cols, tile_weights, tile_count):
    highest = lax.Precision.HIGHEST
    width = features.shape[1]
    row_tiles = N_ROW * NODE_DEV // TILE
    col_tiles = N_COL * NODE_DEV // TILE
    grid_feats = features.reshape(N_COL, N_ROW, NODE_DEV, width)

    def forward_block(col_idx):

        def add_device(row_idx, carry):
            sums, masses = carry
            weights_f = live_weights(tile_weights, tile_count, col_idx, row_idx)
            visible = lax.dynamic_index_in_dim(grid_feats, row_idx, 1, keepdims=False)
            blocks = visible.reshape(col_tiles, TILE, width)[tile_cols[col_idx, row_idx]].astype(jnp.float32)
            products = jnp.einsum('tij,tjf->tif', weights_f, blocks, precision=highest)
            hits = (tile_rows[col_idx, row_idx][None, :] == jnp.arange(row_tiles)[:, None]).astype(jnp.float32)
            partial_value = jnp.einsum('rt,tif->rif', hits, products, precision=highest).reshape(-1, width)
            partial_value = lax.optimization_barrier(partial_value.astype(jnp.bfloat16)).astype(jnp.float32)
            row_mass = jnp.einsum('rt,ti->ri', hits, lax.optimization_barrier(jnp.sum(weights_f, axis=2)), precision=highest).reshape(-1)
            return (sums + partial_value, masses + row_mass)
        start_sums = jnp.zeros((N_ROW * NODE_DEV, width), jnp.float32)
        start_mass = jnp.zeros((N_ROW * NODE_DEV,), jnp.float32)
        return lax.fori_loop(0, N_ROW, add_device, (start_sums, start_mass))
    sums, masses = lax.map(forward_block, jnp.arange(N_COL))
    sums = sums.reshape(NODES, width)
    degree = 1.0 + masses.reshape(NODES)
    aggregate = ((features.astype(jnp.float32) + sums) / degree[:, None]).astype(jnp.bfloat16)
    pre = jnp.dot(aggregate, weight, preferred_element_type=jnp.float32) + bias
    node_out = jax.nn.silu(pre).astype(jnp.bfloat16)
    grad_pre = (grad_out.astype(jnp.float32) * silu_slope(pre)).astype(jnp.bfloat16)
    norm_scale = 1.0 / jnp.sqrt(jnp.float32(NODES))
    grad_weight = jnp.dot(aggregate.T, grad_pre, preferred_element_type=jnp.float32) * norm_scale
    grad_bias = lax.optimization_barrier(jnp.sum(grad_pre.astype(jnp.float32), axis=0)) * norm_scale
    spread = (jnp.dot(grad_pre, weight.T, preferred_element_type=jnp.float32) / degree[:, None]).astype(jnp.bfloat16)
    spread_grid = spread.reshape(N_COL, N_ROW * NODE_DEV, width)

    def backward_device(flat_idx, total):
        col_idx = flat_idx // N_ROW
        row_idx = flat_idx % N_ROW
        weights_f = live_weights(tile_weights, tile_count, col_idx, row_idx)
        owned = lax.dynamic_index_in_dim(spread_grid, col_idx, 0, keepdims=False)
        blocks = owned.reshape(row_tiles, TILE, width)[tile_rows[col_idx, row_idx]].astype(jnp.float32)
        products = jnp.einsum('tij,tif->tjf', weights_f, blocks, precision=highest)
        hits = (tile_cols[col_idx, row_idx][None, :] == jnp.arange(col_tiles)[:, None]).astype(jnp.float32)
        term = jnp.einsum('ct,tjf->cjf', hits, products, precision=highest).reshape(N_COL, NODE_DEV, width)
        term = lax.optimization_barrier(term.astype(jnp.bfloat16)).astype(jnp.float32)
        current = lax.dynamic_index_in_dim(total, row_idx, 1, keepdims=False)
        return lax.dynamic_update_index_in_dim(total, current + term, row_idx, 1)
    start_total = jnp.zeros((N_COL, N_ROW, NODE_DEV, width), jnp.float32)
    total = lax.fori_loop(0, N_COL * N_ROW, backward_device, start_total)
    grad_features = (spread.astype(jnp.float32) + total.reshape(NODES, width)).astype(jnp.bfloat16)
    return (node_out, grad_features, grad_weight, grad_bias)
```

```python
import functools

import jax
import jax.numpy as jnp
from jax import lax
from jax.experimental import pallas as pl
from jax.experimental.pallas import tpu as pltpu
from jax.sharding import Mesh, PartitionSpec as P

AXES = ("x", "zl", "k", "zh", "y")
SIZES = (4, 4, 2, 4, 4)
COL, ROW = ("x", "zl", "k"), ("zh", "y")
TILE, H, EXTRA = 128, 256, 16
PIECE = H // 4
TAIL = PIECE + EXTRA
NORM = 1.0 / 256.0
BF, F32 = jnp.bfloat16, jnp.float32


def call(kernel, outs, in_smem, n_in, scratch=(), flops=1000000):
    vmem = pl.BlockSpec(memory_space=pltpu.VMEM)
    smem = pl.BlockSpec(memory_space=pltpu.SMEM)
    return pl.pallas_call(
        kernel,
        out_shape=outs,
        in_specs=[smem] * in_smem + [vmem] * n_in,
        out_specs=jax.tree.map(lambda _: vmem, outs),
        scratch_shapes=list(scratch),
        compiler_params=pltpu.CompilerParams(vmem_limit_bytes=40 * 1024 * 1024),
        cost_estimate=pl.CostEstimate(flops=flops, bytes_accessed=4000000, transcendentals=0),
    )


def split_rows(total):
    high = total.astype(BF).astype(F32)
    low = total - high
    row = lax.broadcasted_iota(jnp.int32, (EXTRA, H), 0)
    return jnp.where(row == 0, high, jnp.where(row == 1, low, 0.0)).astype(BF)


def sum_ref(ref, count, rows):
    total = ref[0, rows, :].astype(F32)
    for i in range(1, count):
        total += ref[i, rows, :].astype(F32)
    return total


def mass_rows(mass):
    high = mass.astype(BF)
    low = (mass - high.astype(F32)).astype(BF)
    return jnp.concatenate([high, low], axis=1)


def each_slot(count, step):
    def pair(i, carry):
        step(2 * i)
        step(2 * i + 1)
        return carry

    lax.fori_loop(0, count // 2, pair, 0)

    @pl.when(lax.rem(count, 2) == 1)
    def _():
        step(count - 1)


def forward_kernel(rows, cols, count, core, tiles, own, other, out, acc, mass):
    acc[...] = jnp.zeros_like(acc)
    mass[...] = jnp.zeros_like(mass)
    ones = jnp.ones((EXTRA, TILE), BF)

    def step(t):
        tile = tiles[t]
        c, r = cols[0, t], rows[0, t]
        block = jnp.where(lax.rem(c, 2) == core[0], own[c // 2], other[c // 2])
        acc[r] += jnp.dot(tile, block, preferred_element_type=F32)
        mass[r] += lax.dot_general(ones, tile, (((1,), (1,)), ((), ())), preferred_element_type=F32)

    each_slot(count[0, 0], step)
    for r in range(16):
        out[r % 4, r // 4, 0:TILE, :] = acc[r].astype(BF)
        out[r % 4, r // 4, TILE : TILE + EXTRA, :] = mass_rows(mass[r])


def sum_y_kernel(recv, out):
    for z in range(4):
        total = recv[0, z].astype(F32)
        for i in range(1, 4):
            total += recv[i, z].astype(F32)
        out[z, 0:TILE, :] = total[0:TILE].astype(BF)
        ends = total[TILE:]
        out[z, TILE : TILE + EXTRA, :] = mass_rows(ends[:, 0:TILE] + ends[:, TILE:])


def node_kernel(recv, features, grad_out, weight, bias, node_out, spread_out, send):
    total = recv[0].astype(F32) + recv[1].astype(F32) + recv[2].astype(F32) + recv[3].astype(F32)
    ends = total[TILE:]
    mass = 1.0 + ends[0:1, 0:TILE] + ends[0:1, TILE:]
    on_diagonal = lax.broadcasted_iota(jnp.int32, (TILE, TILE), 0) == lax.broadcasted_iota(
        jnp.int32, (TILE, TILE), 1
    )
    degree = jnp.sum(jnp.where(on_diagonal, mass, 0.0), axis=1, keepdims=True)
    aggregate = ((features[...].astype(F32) + total[0:TILE]) / degree).astype(BF)
    w = weight[...]
    pre = jnp.dot(aggregate, w, preferred_element_type=F32) + bias[...]
    sig = jax.nn.sigmoid(pre)
    node_out[...] = (pre * sig).astype(BF)
    grad_pre = (grad_out[...].astype(F32) * (sig * (1.0 + pre * (1.0 - sig)))).astype(BF)
    term = lax.dot_general(
        aggregate, grad_pre, (((0,), (0,)), ((), ())), preferred_element_type=F32
    ).astype(BF)
    bias_rows = split_rows(jnp.sum(grad_pre.astype(F32), axis=0, keepdims=True))
    back = lax.dot_general(grad_pre, w, (((1,), (1,)), ((), ())), preferred_element_type=F32)
    spread = (back / degree).astype(BF)
    spread_out[...] = spread
    for z in range(4):
        send[z, 0:TILE, :] = spread
        send[z, TILE : TILE + PIECE, :] = term[PIECE * z : PIECE * (z + 1)]
        send[z, TILE + PIECE :, :] = bias_rows


def tail_sum(total):
    ends = split_rows(total[PIECE : PIECE + 1] + total[PIECE + 1 : PIECE + 2])
    return jnp.concatenate([total[0:PIECE].astype(BF), ends], axis=0)


def sum_zh_kernel(recv, out):
    tail = tail_sum(sum_ref(recv, 4, slice(TILE, TILE + TAIL)))
    for y in range(4):
        for z in range(4):
            out[y, z * TILE : (z + 1) * TILE, :] = recv[z, 0:TILE, :]
        out[y, 4 * TILE :, :] = tail


def backward_kernel(rows, cols, count, core, tiles, spread, keep, send, acc):
    acc[...] = jnp.zeros_like(acc)

    def step(t):
        c, r = cols[0, t], rows[0, t]
        block = spread[lax.rem(r, 4), pl.ds(pl.multiple_of((r // 4) * TILE, TILE), TILE), :]
        acc[c] += lax.dot_general(
            tiles[t], block, (((0,), (0,)), ((), ())), preferred_element_type=F32
        )

    each_slot(count[0, 0], step)
    me = core[0]
    for i in range(16):
        keep[i * TILE : (i + 1) * TILE, :] = acc[2 * i + me].astype(BF)
        send[i * TILE : (i + 1) * TILE, :] = acc[2 * i + 1 - me].astype(BF)
    tail = tail_sum(sum_ref(spread, 4, slice(4 * TILE, 4 * TILE + TAIL)))
    keep[16 * TILE :, :] = tail
    send[16 * TILE :, :] = tail


def sum_k_kernel(keep, recv, out):
    def both(rows):
        return keep[rows, :].astype(F32) + recv[rows, :].astype(F32)

    tail = tail_sum(both(slice(16 * TILE, 16 * TILE + TAIL)))
    for x in range(4):
        out[x, 0 : 4 * TILE, :] = both(slice(4 * TILE * x, 4 * TILE * (x + 1))).astype(BF)
        out[x, 4 * TILE :, :] = tail


def sum_x_kernel(recv, out):
    tail = tail_sum(sum_ref(recv, 4, slice(4 * TILE, 4 * TILE + TAIL)))
    for z in range(4):
        out[z, 0:TILE, :] = sum_ref(recv, 4, slice(z * TILE, (z + 1) * TILE)).astype(BF)
        out[z, TILE:, :] = tail


def last_kernel(recv, spread, grad_features, piece, grad_bias):
    total = sum_ref(recv, 4, slice(0, TILE))
    grad_features[...] = (spread[...].astype(F32) + total).astype(BF)
    ends = sum_ref(recv, 4, slice(TILE, TILE + TAIL))
    part = ends[0:PIECE].astype(BF)
    for z in range(4):
        piece[z] = part
    grad_bias[...] = (ends[PIECE : PIECE + 1] + ends[PIECE + 1 : PIECE + 2]) * NORM


def exchange(value, axis):
    return lax.all_to_all(value, axis, 0, 0)


def copies(value):
    return jnp.broadcast_to(value[None], (4,) + value.shape)


def shards(features, grad_out, weight, bias, tile_rows, tile_cols, tile_weights, tile_count):
    shape = jax.ShapeDtypeStruct
    rows, cols = tile_rows[0], tile_cols[0]
    tiles = tile_weights[0, 0]
    core = lax.axis_index("k").astype(jnp.int32).reshape(1)
    swap = [(0, 1), (1, 0)]

    own = exchange(copies(features), "zl")
    own = exchange(copies(own), "x").reshape(16, TILE, H)
    other = lax.ppermute(own, "k", swap)
    part = call(
        forward_kernel,
        shape((4, 4, TILE + EXTRA, H), BF),
        4,
        3,
        (pltpu.VMEM((16, TILE, H), F32), pltpu.VMEM((16, EXTRA, TILE), F32)),
        600000000,
    )(rows, cols, tile_count, core, tiles, own, other)
    part = exchange(part, "y")
    part = call(sum_y_kernel, shape((4, TILE + EXTRA, H), BF), 0, 1)(part)
    part = exchange(part, "zh")
    node_out, spread, send = call(
        node_kernel,
        (shape((TILE, H), BF), shape((TILE, H), BF), shape((4, TILE + TAIL, H), BF)),
        0,
        5,
    )(part, features, grad_out, weight, bias.reshape(1, H))
    send = exchange(send, "zh")
    send = call(sum_zh_kernel, shape((4, 4 * TILE + TAIL, H), BF), 0, 1)(send)
    send = exchange(send, "y")
    flat = shape((16 * TILE + TAIL, H), BF)
    keep, away = call(
        backward_kernel, (flat, flat), 4, 2, (pltpu.VMEM((32, TILE, H), F32),), 600000000
    )(rows, cols, tile_count, core, tiles, send)
    back = lax.ppermute(away, "k", swap)
    back = call(sum_k_kernel, shape((4, 4 * TILE + TAIL, H), BF), 0, 2)(keep, back)
    back = exchange(back, "x")
    back = call(sum_x_kernel, shape((4, TILE + TAIL, H), BF), 0, 1)(back)
    back = exchange(back, "zl")
    grad_features, piece, grad_bias = call(
        last_kernel, (shape((TILE, H), BF), shape((4, PIECE, H), BF), shape((1, H), F32)), 0, 2
    )(back, spread)
    grad_weight = exchange(piece, "zh").reshape(H, H).astype(F32) * NORM
    return (node_out, grad_features, grad_weight, grad_bias.reshape(H))


def solution(mesh):
    grid = Mesh(mesh.devices.reshape(SIZES), AXES)
    nodes = P(COL + ROW, None)
    return jax.shard_map(
        shards,
        mesh=grid,
        in_specs=(
            nodes,
            nodes,
            P(),
            P(),
            P(COL, ROW, None),
            P(COL, ROW, None),
            P(COL, ROW, None, None, None),
            P(COL, ROW),
        ),
        out_specs=(nodes, nodes, P(), P()),
        check_vma=False,
    )
```

```python
import functools

import jax
import jax.numpy as jnp
from jax import lax
from jax.experimental import pallas as pl
from jax.experimental.pallas import tpu as pltpu
from jax.sharding import Mesh, PartitionSpec as P

AXES = ("x", "zl", "k", "zh", "y")
SIZES = (4, 4, 2, 4, 4)
COL, ROW = ("x", "zl", "k"), ("zh", "y")
TILE, H, EXTRA = 128, 256, 16
PIECE = H // 4
TAIL = PIECE + EXTRA
NORM = 1.0 / 256.0
BF, F32 = jnp.bfloat16, jnp.float32


def call(kernel, outs, in_smem, n_in, scratch=(), flops=1000000):
    vmem = pl.BlockSpec(memory_space=pltpu.VMEM)
    smem = pl.BlockSpec(memory_space=pltpu.SMEM)
    return pl.pallas_call(
        kernel,
        out_shape=outs,
        in_specs=[smem] * in_smem + [vmem] * n_in,
        out_specs=jax.tree.map(lambda _: vmem, outs),
        scratch_shapes=list(scratch),
        compiler_params=pltpu.CompilerParams(vmem_limit_bytes=40 * 1024 * 1024),
        cost_estimate=pl.CostEstimate(flops=flops, bytes_accessed=4000000, transcendentals=0),
    )


def split_rows(total):
    high = total.astype(BF).astype(F32)
    low = total - high
    row = lax.broadcasted_iota(jnp.int32, (EXTRA, H), 0)
    return jnp.where(row == 0, high, jnp.where(row == 1, low, 0.0)).astype(BF)


def sum_ref(ref, count, rows):
    total = ref[0, rows, :].astype(F32)
    for i in range(1, count):
        total += ref[i, rows, :].astype(F32)
    return total


def mass_rows(mass):
    high = mass.astype(BF)
    low = (mass - high.astype(F32)).astype(BF)
    return jnp.concatenate([high, low], axis=1)


def each_slot(count, step):
    def pair(i, carry):
        step(2 * i)
        step(2 * i + 1)
        return carry

    lax.fori_loop(0, count // 2, pair, 0)

    @pl.when(lax.rem(count, 2) == 1)
    def _():
        step(count - 1)


def add_block(acc, seen, i, product):
    acc[i] = jnp.where(seen[i] == 1, acc[i], 0.0) + product
    seen[i] = 1


def clear(seen, count):
    for i in range(count):
        seen[i] = 0


def forward_kernel(rows, cols, count, core, tiles, own, other, out, acc, mass, seen):
    clear(seen, 16)
    mass[...] = jnp.zeros_like(mass)
    ones = jnp.ones((EXTRA, TILE), BF)

    def step(t):
        tile = tiles[t]
        c, r = cols[0, t], rows[0, t]
        block = jnp.where(lax.rem(c, 2) == core[0], own[c // 2], other[c // 2])
        add_block(acc, seen, r, jnp.dot(tile, block, preferred_element_type=F32))
        mass[r] += lax.dot_general(ones, tile, (((1,), (1,)), ((), ())), preferred_element_type=F32)

    each_slot(count[0, 0], step)
    for r in range(16):
        out[r % 4, r // 4, 0:TILE, :] = jnp.where(seen[r] == 1, acc[r], 0.0).astype(BF)
        out[r % 4, r // 4, TILE : TILE + EXTRA, :] = mass_rows(mass[r])


def sum_y_kernel(recv, out):
    for z in range(4):
        total = recv[0, z].astype(F32)
        for i in range(1, 4):
            total += recv[i, z].astype(F32)
        out[z, 0:TILE, :] = total[0:TILE].astype(BF)
        ends = total[TILE:]
        out[z, TILE : TILE + EXTRA, :] = mass_rows(ends[:, 0:TILE] + ends[:, TILE:])


def column(lanes):
    on_diagonal = lax.broadcasted_iota(jnp.int32, (TILE, TILE), 0) == lax.broadcasted_iota(
        jnp.int32, (TILE, TILE), 1
    )
    return jnp.sum(jnp.where(on_diagonal, lanes, 0.0), axis=1, keepdims=True)


def node_kernel(recv, features, grad_out, weight, bias, node_out, spread_out, send):
    total = recv[0].astype(F32) + recv[1].astype(F32) + recv[2].astype(F32) + recv[3].astype(F32)
    ends = total[TILE:]
    degrees = 1.0 + ends[:, 0:TILE] + ends[:, TILE:]
    degree = column(degrees[0:1])
    aggregate = ((features[...].astype(F32) + total[0:TILE]) / degree).astype(BF)
    w = weight[...]
    pre = jnp.dot(aggregate, w, preferred_element_type=F32) + bias[...]
    sig = jax.nn.sigmoid(pre)
    node_out[...] = (pre * sig).astype(BF)
    grad_pre = (grad_out[...].astype(F32) * (sig * (1.0 + pre * (1.0 - sig)))).astype(BF)
    back = lax.dot_general(grad_pre, w, (((1,), (1,)), ((), ())), preferred_element_type=F32)
    spread_out[...] = (back / degree).astype(BF)
    degree_rows = mass_rows(degrees)
    for z in range(4):
        send[z, 0:TILE, :] = grad_pre
        send[z, TILE : 2 * TILE, :] = aggregate
        send[z, 2 * TILE :, :] = degree_rows


def four_kernel(recv, weight, out):
    w = weight[...]
    term = jnp.zeros((H, H), F32)
    bias_term = jnp.zeros((1, H), F32)
    for z in range(4):
        grad_pre = recv[z, 0:TILE, :]
        aggregate = recv[z, TILE : 2 * TILE, :]
        ends = recv[z, 2 * TILE :, :].astype(F32)
        degree = column(ends[0:1, 0:TILE] + ends[0:1, TILE:])
        back = lax.dot_general(grad_pre, w, (((1,), (1,)), ((), ())), preferred_element_type=F32)
        spread = (back / degree).astype(BF)
        for y in range(4):
            out[y, z * TILE : (z + 1) * TILE, :] = spread
        term += lax.dot_general(
            aggregate, grad_pre, (((0,), (0,)), ((), ())), preferred_element_type=F32
        )
        bias_term += jnp.sum(grad_pre.astype(F32), axis=0, keepdims=True)
    bias_rows = split_rows(bias_term)
    for y in range(4):
        out[y, 4 * TILE : 4 * TILE + PIECE, :] = term[PIECE * y : PIECE * (y + 1)].astype(BF)
        out[y, 4 * TILE + PIECE :, :] = bias_rows


def tail_sum(total):
    ends = split_rows(total[PIECE : PIECE + 1] + total[PIECE + 1 : PIECE + 2])
    return jnp.concatenate([total[0:PIECE].astype(BF), ends], axis=0)


def backward_kernel(rows, cols, count, core, tiles, spread, keep, send, acc, seen):
    clear(seen, 32)

    def step(t):
        c, r = cols[0, t], rows[0, t]
        block = spread[lax.rem(r, 4), pl.ds(pl.multiple_of((r // 4) * TILE, TILE), TILE), :]
        product = lax.dot_general(
            tiles[t], block, (((0,), (0,)), ((), ())), preferred_element_type=F32
        )
        add_block(acc, seen, c, product)

    each_slot(count[0, 0], step)
    me = core[0]
    for i in range(16):
        mine, others = 2 * i + me, 2 * i + 1 - me
        here = slice(i * TILE, (i + 1) * TILE)
        keep[here, :] = jnp.where(seen[mine] == 1, acc[mine], 0.0).astype(BF)
        send[here, :] = jnp.where(seen[others] == 1, acc[others], 0.0).astype(BF)
    tail = tail_sum(sum_ref(spread, 4, slice(4 * TILE, 4 * TILE + TAIL)))
    keep[16 * TILE :, :] = tail
    send[16 * TILE :, :] = tail


def sum_k_kernel(core, keep, recv, out):
    def both(rows):
        return keep[rows, :].astype(F32) + recv[rows, :].astype(F32)

    tail = tail_sum(both(slice(16 * TILE, 16 * TILE + TAIL)))
    first = core[0] == 0
    for d in range(4):
        for e in range(4):
            i = jnp.where(first, 4 * d + e, 4 * e + d)
            rows = pl.ds(pl.multiple_of(i * TILE, TILE), TILE)
            out[d, e * TILE : (e + 1) * TILE, :] = both(rows).astype(BF)
        out[d, 4 * TILE :, :] = tail


def sum_x_kernel(recv, out):
    tail = tail_sum(sum_ref(recv, 4, slice(4 * TILE, 4 * TILE + TAIL)))
    for z in range(4):
        out[z, 0:TILE, :] = sum_ref(recv, 4, slice(z * TILE, (z + 1) * TILE)).astype(BF)
        out[z, TILE:, :] = tail


def last_kernel(recv, spread, grad_features):
    total = sum_ref(recv, 4, slice(0, TILE))
    grad_features[...] = (spread[...].astype(F32) + total).astype(BF)


def piece_kernel(recv, piece, grad_bias):
    ends = sum_ref(recv, 4, slice(TILE, TILE + TAIL))
    part = ends[0:PIECE].astype(BF)
    for y in range(4):
        piece[y] = part
    grad_bias[...] = (ends[PIECE : PIECE + 1] + ends[PIECE + 1 : PIECE + 2]) * NORM


def exchange(value, axis):
    return lax.all_to_all(value, axis, 0, 0)


ALONG_X = [[[(x * 4 + z) * 2 + k for x in range(4)] for z in range(4)] for k in range(2)]
ALONG_Z = [[[(x * 4 + z) * 2 + k for z in range(4)] for x in range(4)] for k in range(2)]
FIRST = ALONG_X[0] + ALONG_Z[1]
SECOND = ALONG_Z[0] + ALONG_X[1]


def exchange_col(value, groups):
    return lax.all_to_all(value, COL, 0, 0, axis_index_groups=groups)


def copies(value):
    return jnp.broadcast_to(value[None], (4,) + value.shape)


def shards(features, grad_out, weight, bias, tile_rows, tile_cols, tile_weights, tile_count):
    shape = jax.ShapeDtypeStruct
    rows, cols = tile_rows[0], tile_cols[0]
    tiles = tile_weights[0, 0]
    core = lax.axis_index("k").astype(jnp.int32).reshape(1)
    swap = [(0, 1), (1, 0)]

    own = exchange(copies(features), "zl")
    own = exchange(copies(own), "x").reshape(16, TILE, H)
    other = lax.ppermute(own, "k", swap)
    part = call(
        forward_kernel,
        shape((4, 4, TILE + EXTRA, H), BF),
        4,
        3,
        (pltpu.VMEM((16, TILE, H), F32), pltpu.VMEM((16, EXTRA, TILE), F32), pltpu.SMEM((16,), jnp.int32)),
        600000000,
    )(rows, cols, tile_count, core, tiles, own, other)
    part = exchange(part, "y")
    part = call(sum_y_kernel, shape((4, TILE + EXTRA, H), BF), 0, 1)(part)
    part = exchange(part, "zh")
    node_out, spread, send = call(
        node_kernel,
        (shape((TILE, H), BF), shape((TILE, H), BF), shape((4, 2 * TILE + EXTRA, H), BF)),
        0,
        5,
    )(part, features, grad_out, weight, bias.reshape(1, H))
    send = exchange(send, "zh")
    send = call(four_kernel, shape((4, 4 * TILE + TAIL, H), BF), 0, 2)(send, weight)
    send = exchange(send, "y")
    flat = shape((16 * TILE + TAIL, H), BF)
    keep, away = call(
        backward_kernel, (flat, flat), 4, 2, (pltpu.VMEM((32, TILE, H), F32), pltpu.SMEM((32,), jnp.int32)), 600000000
    )(rows, cols, tile_count, core, tiles, send)
    back = lax.ppermute(away, "k", swap)
    back = call(sum_k_kernel, shape((4, 4 * TILE + TAIL, H), BF), 1, 2)(
        core, keep, back
    )
    back = exchange_col(back, FIRST)
    back = call(sum_x_kernel, shape((4, TILE + TAIL, H), BF), 0, 1)(back)
    back = exchange_col(back, SECOND)
    piece, grad_bias = call(
        piece_kernel, (shape((4, PIECE, H), BF), shape((1, H), F32)), 0, 1
    )(back)
    grad_weight = exchange(piece, "y").reshape(H, H).astype(F32) * NORM
    grad_features = call(last_kernel, shape((TILE, H), BF), 0, 2)(back, spread)
    return (node_out, grad_features, grad_weight, grad_bias.reshape(H))


def solution(mesh):
    grid = Mesh(mesh.devices.reshape(SIZES), AXES)
    nodes = P(COL + ROW, None)
    return jax.shard_map(
        shards,
        mesh=grid,
        in_specs=(
            nodes,
            nodes,
            P(),
            P(),
            P(COL, ROW, None),
            P(COL, ROW, None),
            P(COL, ROW, None, None, None),
            P(COL, ROW),
        ),
        out_specs=(nodes, nodes, P(), P()),
        check_vma=False,
    )
```

```python
import functools

import jax
import jax.numpy as jnp
from jax import lax
from jax.experimental import pallas as pl
from jax.experimental.pallas import tpu as pltpu
from jax.sharding import Mesh, PartitionSpec as P

AXES = ("x", "zl", "k", "zh", "y")
SIZES = (4, 4, 2, 4, 4)
COL, ROW = ("x", "zl", "k"), ("zh", "y")
TILE, H, EXTRA = 128, 256, 16
PIECE = H // 4
TAIL = PIECE + EXTRA
NORM = 1.0 / 256.0
BF, F32 = jnp.bfloat16, jnp.float32


def call(kernel, outs, in_smem, n_in, scratch=(), flops=1000000):
    vmem = pl.BlockSpec(memory_space=pltpu.VMEM)
    smem = pl.BlockSpec(memory_space=pltpu.SMEM)
    return pl.pallas_call(
        kernel,
        out_shape=outs,
        in_specs=[smem] * in_smem + [vmem] * n_in,
        out_specs=jax.tree.map(lambda _: vmem, outs),
        scratch_shapes=list(scratch),
        compiler_params=pltpu.CompilerParams(vmem_limit_bytes=40 * 1024 * 1024),
        cost_estimate=pl.CostEstimate(flops=flops, bytes_accessed=4000000, transcendentals=0),
    )


def split_rows(total):
    high = total.astype(BF).astype(F32)
    low = total - high
    row = lax.broadcasted_iota(jnp.int32, (EXTRA, H), 0)
    return jnp.where(row == 0, high, jnp.where(row == 1, low, 0.0)).astype(BF)


def sum_ref(ref, count, rows):
    total = ref[0, rows, :].astype(F32)
    for i in range(1, count):
        total += ref[i, rows, :].astype(F32)
    return total


def mass_rows(mass):
    high = mass.astype(BF)
    low = (mass - high.astype(F32)).astype(BF)
    return jnp.concatenate([high, low], axis=1)


def each_slot(count, step):
    def pair(i, carry):
        step(2 * i)
        step(2 * i + 1)
        return carry

    lax.fori_loop(0, count // 2, pair, 0)

    @pl.when(lax.rem(count, 2) == 1)
    def _():
        step(count - 1)


def add_block(acc, seen, i, product):
    acc[i] = jnp.where(seen[i] == 1, acc[i], 0.0) + product
    seen[i] = 1


def clear(seen, count):
    for i in range(count):
        seen[i] = 0


def forward_kernel(
    rows, cols, count, core, zh, y, tiles, own, other, far, near1, near2, near3, mine, acc, mass, seen
):
    clear(seen, 16)
    mass[...] = jnp.zeros_like(mass)
    ones = jnp.ones((EXTRA, TILE), BF)

    def step(t):
        tile = tiles[t]
        c, r = cols[0, t], rows[0, t]
        block = jnp.where(lax.rem(c, 2) == core[0], own[c // 2], other[c // 2])
        add_block(acc, seen, r, jnp.dot(tile, block, preferred_element_type=F32))
        mass[r] += lax.dot_general(ones, tile, (((1,), (1,)), ((), ())), preferred_element_type=F32)

    each_slot(count[0, 0], step)

    def put(out, r):
        out[0:TILE, :] = jnp.where(seen[r] == 1, acc[r], 0.0).astype(BF)
        out[TILE : TILE + EXTRA, :] = mass_rows(mass[r])

    for d in (1, 2, 3):
        for to in range(4):
            put(far.at[to, d - 1], 4 * lax.rem(zh[0] + d, 4) + to)
    for d, out in enumerate((mine, near1, near2, near3)):
        put(out, 4 * zh[0] + lax.rem(y[0] + d, 4))


def sum_y_kernel(zh, recv, out):
    out[zh[0]] = jnp.zeros((TILE + EXTRA, H), BF)
    for d in (1, 2, 3):
        total = recv[0, d - 1].astype(F32)
        for i in range(1, 4):
            total += recv[i, d - 1].astype(F32)
        z = lax.rem(zh[0] + d, 4)
        out[z, 0:TILE, :] = total[0:TILE].astype(BF)
        ends = total[TILE:]
        out[z, TILE : TILE + EXTRA, :] = mass_rows(ends[:, 0:TILE] + ends[:, TILE:])


def column(lanes):
    on_diagonal = lax.broadcasted_iota(jnp.int32, (TILE, TILE), 0) == lax.broadcasted_iota(
        jnp.int32, (TILE, TILE), 1
    )
    return jnp.sum(jnp.where(on_diagonal, lanes, 0.0), axis=1, keepdims=True)


def node_kernel(
    recv, mine, near1, near2, near3, features, grad_out, weight, bias, node_out, spread_out, send
):
    total = mine[...].astype(F32) + recv[0].astype(F32)
    for block in (recv[1], recv[2], recv[3], near1[...], near2[...], near3[...]):
        total += block.astype(F32)
    ends = total[TILE:]
    degrees = 1.0 + ends[:, 0:TILE] + ends[:, TILE:]
    degree = column(degrees[0:1])
    aggregate = ((features[...].astype(F32) + total[0:TILE]) / degree).astype(BF)
    w = weight[...]
    pre = jnp.dot(aggregate, w, preferred_element_type=F32) + bias[...]
    sig = jax.nn.sigmoid(pre)
    node_out[...] = (pre * sig).astype(BF)
    grad_pre = (grad_out[...].astype(F32) * (sig * (1.0 + pre * (1.0 - sig)))).astype(BF)
    back = lax.dot_general(grad_pre, w, (((1,), (1,)), ((), ())), preferred_element_type=F32)
    spread_out[...] = (back / degree).astype(BF)
    degree_rows = mass_rows(degrees)
    for z in range(4):
        send[z, 0:TILE, :] = grad_pre
        send[z, TILE : 2 * TILE, :] = aggregate
        send[z, 2 * TILE :, :] = degree_rows


def four_kernel(zh, recv, weight, out):
    w = weight[...]
    for d in (1, 2, 3):
        z = lax.rem(zh[0] + d, 4)
        ends = recv[z, 2 * TILE :, :].astype(F32)
        degree = column(ends[0:1, 0:TILE] + ends[0:1, TILE:])
        back = lax.dot_general(
            recv[z, 0:TILE, :], w, (((1,), (1,)), ((), ())), preferred_element_type=F32
        )
        spread = (back / degree).astype(BF)
        for y in range(4):
            out[y, (d - 1) * TILE : d * TILE, :] = spread
    term = jnp.zeros((H, H), F32)
    bias_term = jnp.zeros((1, H), F32)
    for z in range(4):
        grad_pre = recv[z, 0:TILE, :]
        term += lax.dot_general(
            recv[z, TILE : 2 * TILE, :],
            grad_pre,
            (((0,), (0,)), ((), ())),
            preferred_element_type=F32,
        )
        bias_term += jnp.sum(grad_pre.astype(F32), axis=0, keepdims=True)
    bias_rows = split_rows(bias_term)
    for y in range(4):
        out[y, 3 * TILE : 3 * TILE + PIECE, :] = term[PIECE * y : PIECE * (y + 1)].astype(BF)
        out[y, 3 * TILE + PIECE :, :] = bias_rows


def tail_sum(total):
    ends = split_rows(total[PIECE : PIECE + 1] + total[PIECE + 1 : PIECE + 2])
    return jnp.concatenate([total[0:PIECE].astype(BF), ends], axis=0)


def backward_kernel(
    rows, cols, count, core, zh, y, tiles, far, mine, near1, near2, near3, keep, send, near, acc, seen
):
    clear(seen, 32)
    for d, block in enumerate((mine, near1, near2, near3)):
        near[lax.rem(y[0] + 4 - d, 4)] = block[...]

    def step(t):
        c, r = cols[0, t], rows[0, t]
        d = lax.rem(r // 4 + 4 - zh[0], 4)
        start = pl.multiple_of(jnp.maximum(d - 1, 0) * TILE, TILE)
        at_y = lax.rem(r, 4)
        block = jnp.where(d == 0, near[at_y], far[at_y, pl.ds(start, TILE), :])
        product = lax.dot_general(
            tiles[t], block, (((0,), (0,)), ((), ())), preferred_element_type=F32
        )
        add_block(acc, seen, c, product)

    each_slot(count[0, 0], step)
    me = core[0]
    for i in range(16):
        mine, others = 2 * i + me, 2 * i + 1 - me
        here = slice(i * TILE, (i + 1) * TILE)
        keep[here, :] = jnp.where(seen[mine] == 1, acc[mine], 0.0).astype(BF)
        send[here, :] = jnp.where(seen[others] == 1, acc[others], 0.0).astype(BF)
    tail = tail_sum(sum_ref(far, 4, slice(3 * TILE, 3 * TILE + TAIL)))
    keep[16 * TILE :, :] = tail
    send[16 * TILE :, :] = tail


def sum_k_kernel(core, keep, recv, out):
    def both(rows):
        return keep[rows, :].astype(F32) + recv[rows, :].astype(F32)

    tail = tail_sum(both(slice(16 * TILE, 16 * TILE + TAIL)))
    first = core[0] == 0
    for d in range(4):
        for e in range(4):
            i = jnp.where(first, 4 * d + e, 4 * e + d)
            rows = pl.ds(pl.multiple_of(i * TILE, TILE), TILE)
            out[d, e * TILE : (e + 1) * TILE, :] = both(rows).astype(BF)
        out[d, 4 * TILE :, :] = tail


def sum_x_kernel(recv, out):
    tail = tail_sum(sum_ref(recv, 4, slice(4 * TILE, 4 * TILE + TAIL)))
    for z in range(4):
        out[z, 0:TILE, :] = sum_ref(recv, 4, slice(z * TILE, (z + 1) * TILE)).astype(BF)
        out[z, TILE:, :] = tail


def last_kernel(recv, spread, grad_features):
    total = sum_ref(recv, 4, slice(0, TILE))
    grad_features[...] = (spread[...].astype(F32) + total).astype(BF)


def piece_kernel(recv, piece, grad_bias):
    ends = sum_ref(recv, 4, slice(TILE, TILE + TAIL))
    part = ends[0:PIECE].astype(BF)
    for y in range(4):
        piece[y] = part
    grad_bias[...] = (ends[PIECE : PIECE + 1] + ends[PIECE + 1 : PIECE + 2]) * NORM


def exchange(value, axis):
    return lax.all_to_all(value, axis, 0, 0)


ALONG_X = [[[(x * 4 + z) * 2 + k for x in range(4)] for z in range(4)] for k in range(2)]
ALONG_Z = [[[(x * 4 + z) * 2 + k for z in range(4)] for x in range(4)] for k in range(2)]
FIRST = ALONG_X[0] + ALONG_Z[1]
SECOND = ALONG_Z[0] + ALONG_X[1]


def exchange_col(value, groups):
    return lax.all_to_all(value, COL, 0, 0, axis_index_groups=groups)


def along_y(*blocks):
    return [
        lax.ppermute(block, "y", [(i, (i + d) % 4) for i in range(4)])
        for d, block in enumerate(blocks, 1)
    ]


def copies(value):
    return jnp.broadcast_to(value[None], (4,) + value.shape)


def shards(features, grad_out, weight, bias, tile_rows, tile_cols, tile_weights, tile_count):
    shape = jax.ShapeDtypeStruct
    rows, cols = tile_rows[0], tile_cols[0]
    tiles = tile_weights[0, 0]
    core, zh, y = (lax.axis_index(a).astype(jnp.int32).reshape(1) for a in ("k", "zh", "y"))
    swap = [(0, 1), (1, 0)]

    own = exchange(copies(features), "zl")
    own = exchange(copies(own), "x").reshape(16, TILE, H)
    other = lax.ppermute(own, "k", swap)
    one_block = shape((TILE + EXTRA, H), BF)
    part, near1, near2, near3, mine = call(
        forward_kernel,
        (shape((4, 3, TILE + EXTRA, H), BF),) + (one_block,) * 4,
        6,
        3,
        (
            pltpu.VMEM((16, TILE, H), F32),
            pltpu.VMEM((16, EXTRA, TILE), F32),
            pltpu.SMEM((16,), jnp.int32),
        ),
        600000000,
    )(rows, cols, tile_count, core, zh, y, tiles, own, other)
    part = exchange(part, "y")
    part = call(sum_y_kernel, shape((4, TILE + EXTRA, H), BF), 1, 1)(zh, part)
    part = exchange(part, "zh")
    near = along_y(near1, near2, near3)
    node_out, spread, send = call(
        node_kernel,
        (shape((TILE, H), BF), shape((TILE, H), BF), shape((4, 2 * TILE + EXTRA, H), BF)),
        0,
        9,
    )(part, mine, *near, features, grad_out, weight, bias.reshape(1, H))
    send = exchange(send, "zh")
    send, *near = lax.optimization_barrier([send, *along_y(spread, spread, spread)])
    send = call(four_kernel, shape((4, 3 * TILE + TAIL, H), BF), 1, 2)(zh, send, weight)
    send = exchange(send, "y")
    flat = shape((16 * TILE + TAIL, H), BF)
    keep, away = call(
        backward_kernel,
        (flat, flat),
        6,
        6,
        (
            pltpu.VMEM((4, TILE, H), BF),
            pltpu.VMEM((32, TILE, H), F32),
            pltpu.SMEM((32,), jnp.int32),
        ),
        600000000,
    )(rows, cols, tile_count, core, zh, y, tiles, send, spread, *near)
    back = lax.ppermute(away, "k", swap)
    back = call(sum_k_kernel, shape((4, 4 * TILE + TAIL, H), BF), 1, 2)(
        core, keep, back
    )
    back = exchange_col(back, FIRST)
    back = call(sum_x_kernel, shape((4, TILE + TAIL, H), BF), 0, 1)(back)
    back = exchange_col(back, SECOND)
    piece, grad_bias = call(
        piece_kernel, (shape((4, PIECE, H), BF), shape((1, H), F32)), 0, 1
    )(back)
    grad_weight = exchange(piece, "y").reshape(H, H).astype(F32) * NORM
    grad_features = call(last_kernel, shape((TILE, H), BF), 0, 2)(back, spread)
    return (node_out, grad_features, grad_weight, grad_bias.reshape(H))


def solution(mesh):
    grid = Mesh(mesh.devices.reshape(SIZES), AXES)
    nodes = P(COL + ROW, None)
    return jax.shard_map(
        shards,
        mesh=grid,
        in_specs=(
            nodes,
            nodes,
            P(),
            P(),
            P(COL, ROW, None),
            P(COL, ROW, None),
            P(COL, ROW, None, None, None),
            P(COL, ROW),
        ),
        out_specs=(nodes, nodes, P(), P()),
        check_vma=False,
    )
```

```python
import functools

import jax
import jax.numpy as jnp
from jax import lax
from jax.experimental import pallas as pl
from jax.experimental.pallas import tpu as pltpu
from jax.sharding import Mesh, PartitionSpec as P

AXES = ("x", "zl", "k", "zh", "y")
SIZES = (4, 4, 2, 4, 4)
COL, ROW = ("x", "zl", "k"), ("zh", "y")
TILE, H, EXTRA = 128, 256, 16
PIECE = H // 4
TAIL = PIECE + EXTRA
NORM = 1.0 / 256.0
BF, F32 = jnp.bfloat16, jnp.float32


def call(kernel, outs, in_smem, n_in, scratch=(), flops=1000000):
    vmem = pl.BlockSpec(memory_space=pltpu.VMEM)
    smem = pl.BlockSpec(memory_space=pltpu.SMEM)
    return pl.pallas_call(
        kernel,
        out_shape=outs,
        in_specs=[smem] * in_smem + [vmem] * n_in,
        out_specs=jax.tree.map(lambda _: vmem, outs),
        scratch_shapes=list(scratch),
        compiler_params=pltpu.CompilerParams(vmem_limit_bytes=40 * 1024 * 1024),
        cost_estimate=pl.CostEstimate(flops=flops, bytes_accessed=4000000, transcendentals=0),
    )


def split_rows(total):
    high = total.astype(BF).astype(F32)
    low = total - high
    row = lax.broadcasted_iota(jnp.int32, (EXTRA, H), 0)
    return jnp.where(row == 0, high, jnp.where(row == 1, low, 0.0)).astype(BF)


def sum_ref(ref, count, rows):
    total = ref[0, rows, :].astype(F32)
    for i in range(1, count):
        total += ref[i, rows, :].astype(F32)
    return total


def mass_rows(mass):
    high = mass.astype(BF)
    low = (mass - high.astype(F32)).astype(BF)
    return jnp.concatenate([high, low], axis=1)


def each_slot(count, step):
    def pair(i, carry):
        step(2 * i)
        step(2 * i + 1)
        return carry

    lax.fori_loop(0, count // 2, pair, 0)

    @pl.when(lax.rem(count, 2) == 1)
    def _():
        step(count - 1)


def clear(seen, count):
    for i in range(count):
        seen[i] = 0


def slots_of(cols, count, parity, order):
    def put(t, n):
        order[n] = t
        return n + jnp.where(lax.rem(cols[0, t], 2) == parity, 1, 0)

    return lax.fori_loop(0, count, put, 0)


def row_sums(ones, tile):
    return lax.dot_general(ones, tile, (((1,), (1,)), ((), ())), preferred_element_type=F32)


def own_kernel(rows, cols, count, core, tiles, own, begun, mass, seen, order):
    clear(seen, 16)
    mass[...] = jnp.zeros_like(mass)
    ones = jnp.ones((EXTRA, TILE), BF)

    def step(i):
        t = order[i]
        r = rows[0, t]
        tile = tiles[t]
        product = jnp.dot(tile, own[cols[0, t] // 2], preferred_element_type=F32)
        begun[r] = jnp.where(seen[r] == 1, begun[r], 0.0) + product
        mass[r] += row_sums(ones, tile)
        seen[r] = 1

    each_slot(slots_of(cols, count[0, 0], core[0], order), step)


def forward_kernel(
    rows, cols, count, core, zh, y, tiles, other, begun, masses, far, near1, near2, near3, mine, acc, mass, seen, order
):
    clear(seen, 16)
    mass[...] = masses[...]
    ones = jnp.ones((EXTRA, TILE), BF)

    def mark(i, carry):
        seen[rows[0, order[i]]] = 1
        return carry

    lax.fori_loop(0, slots_of(cols, count[0, 0], core[0], order), mark, 0)

    def so_far(r):
        return jnp.where(seen[r] == 2, acc[r], jnp.where(seen[r] == 1, begun[r], 0.0))

    def step(i):
        t = order[i]
        r = rows[0, t]
        tile = tiles[t]
        acc[r] = so_far(r) + jnp.dot(tile, other[cols[0, t] // 2], preferred_element_type=F32)
        mass[r] += row_sums(ones, tile)
        seen[r] = 2

    each_slot(slots_of(cols, count[0, 0], 1 - core[0], order), step)

    def put(out, r):
        out[0:TILE, :] = so_far(r).astype(BF)
        out[TILE : TILE + EXTRA, :] = mass_rows(mass[r])

    for d in (1, 2, 3):
        for to in range(4):
            put(far.at[to, d - 1], 4 * lax.rem(zh[0] + d, 4) + to)
    for d, out in enumerate((mine, near1, near2, near3)):
        put(out, 4 * zh[0] + lax.rem(y[0] + d, 4))


def sum_y_kernel(zh, recv, out):
    out[zh[0]] = jnp.zeros((TILE + EXTRA, H), BF)
    for d in (1, 2, 3):
        total = recv[0, d - 1].astype(F32)
        for i in range(1, 4):
            total += recv[i, d - 1].astype(F32)
        z = lax.rem(zh[0] + d, 4)
        out[z, 0:TILE, :] = total[0:TILE].astype(BF)
        ends = total[TILE:]
        out[z, TILE : TILE + EXTRA, :] = mass_rows(ends[:, 0:TILE] + ends[:, TILE:])


def column(lanes):
    on_diagonal = lax.broadcasted_iota(jnp.int32, (TILE, TILE), 0) == lax.broadcasted_iota(
        jnp.int32, (TILE, TILE), 1
    )
    return jnp.sum(jnp.where(on_diagonal, lanes, 0.0), axis=1, keepdims=True)


def node_kernel(
    recv, mine, near1, near2, near3, features, grad_out, weight, bias, node_out, spread_out, send
):
    total = mine[...].astype(F32) + recv[0].astype(F32)
    for block in (recv[1], recv[2], recv[3], near1[...], near2[...], near3[...]):
        total += block.astype(F32)
    ends = total[TILE:]
    degrees = 1.0 + ends[:, 0:TILE] + ends[:, TILE:]
    degree = column(degrees[0:1])
    aggregate = ((features[...].astype(F32) + total[0:TILE]) / degree).astype(BF)
    w = weight[...]
    pre = jnp.dot(aggregate, w, preferred_element_type=F32) + bias[...]
    sig = jax.nn.sigmoid(pre)
    node_out[...] = (pre * sig).astype(BF)
    grad_pre = (grad_out[...].astype(F32) * (sig * (1.0 + pre * (1.0 - sig)))).astype(BF)
    back = lax.dot_general(grad_pre, w, (((1,), (1,)), ((), ())), preferred_element_type=F32)
    spread_out[...] = (back / degree).astype(BF)
    degree_rows = mass_rows(degrees)
    for z in range(4):
        send[z, 0:TILE, :] = grad_pre
        send[z, TILE : 2 * TILE, :] = aggregate
        send[z, 2 * TILE :, :] = degree_rows


def four_kernel(zh, recv, weight, out):
    w = weight[...]
    for d in (1, 2, 3):
        z = lax.rem(zh[0] + d, 4)
        ends = recv[z, 2 * TILE :, :].astype(F32)
        degree = column(ends[0:1, 0:TILE] + ends[0:1, TILE:])
        back = lax.dot_general(
            recv[z, 0:TILE, :], w, (((1,), (1,)), ((), ())), preferred_element_type=F32
        )
        spread = (back / degree).astype(BF)
        for y in range(4):
            out[y, (d - 1) * TILE : d * TILE, :] = spread
    term = jnp.zeros((H, H), F32)
    bias_term = jnp.zeros((1, H), F32)
    for z in range(4):
        grad_pre = recv[z, 0:TILE, :]
        term += lax.dot_general(
            recv[z, TILE : 2 * TILE, :],
            grad_pre,
            (((0,), (0,)), ((), ())),
            preferred_element_type=F32,
        )
        bias_term += jnp.sum(grad_pre.astype(F32), axis=0, keepdims=True)
    bias_rows = split_rows(bias_term)
    for y in range(4):
        out[y, 3 * TILE : 3 * TILE + PIECE, :] = term[PIECE * y : PIECE * (y + 1)].astype(BF)
        out[y, 3 * TILE + PIECE :, :] = bias_rows


def tail_sum(total):
    ends = split_rows(total[PIECE : PIECE + 1] + total[PIECE + 1 : PIECE + 2])
    return jnp.concatenate([total[0:PIECE].astype(BF), ends], axis=0)


def backward_kernel(
    flip, rows, cols, count, core, zh, y, tiles, far, mine, near1, near2, near3, out, near, acc, seen, order
):
    clear(seen, 16)
    for d, block in enumerate((mine, near1, near2, near3)):
        near[lax.rem(y[0] + 4 - d, 4)] = block[...]
    parity = 1 - core[0] if flip else core[0]

    def step(i):
        t = order[i]
        c, r = cols[0, t] // 2, rows[0, t]
        d = lax.rem(r // 4 + 4 - zh[0], 4)
        start = pl.multiple_of(jnp.maximum(d - 1, 0) * TILE, TILE)
        at_y = lax.rem(r, 4)
        block = jnp.where(d == 0, near[at_y], far[at_y, pl.ds(start, TILE), :])
        product = lax.dot_general(
            tiles[t], block, (((0,), (0,)), ((), ())), preferred_element_type=F32
        )
        acc[c] = jnp.where(seen[c] == 1, acc[c], 0.0) + product
        seen[c] = 1

    each_slot(slots_of(cols, count[0, 0], parity, order), step)
    for i in range(16):
        out[i * TILE : (i + 1) * TILE, :] = jnp.where(seen[i] == 1, acc[i], 0.0).astype(BF)
    out[16 * TILE :, :] = tail_sum(sum_ref(far, 4, slice(3 * TILE, 3 * TILE + TAIL)))


def sum_k_kernel(core, keep, recv, out):
    def both(rows):
        return keep[rows, :].astype(F32) + recv[rows, :].astype(F32)

    tail = tail_sum(both(slice(16 * TILE, 16 * TILE + TAIL)))
    first = core[0] == 0
    for d in range(4):
        for e in range(4):
            i = jnp.where(first, 4 * d + e, 4 * e + d)
            rows = pl.ds(pl.multiple_of(i * TILE, TILE), TILE)
            out[d, e * TILE : (e + 1) * TILE, :] = both(rows).astype(BF)
        out[d, 4 * TILE :, :] = tail


def sum_x_kernel(recv, out):
    tail = tail_sum(sum_ref(recv, 4, slice(4 * TILE, 4 * TILE + TAIL)))
    for z in range(4):
        out[z, 0:TILE, :] = sum_ref(recv, 4, slice(z * TILE, (z + 1) * TILE)).astype(BF)
        out[z, TILE:, :] = tail


def last_kernel(recv, spread, grad_features, piece, grad_bias):
    total = sum_ref(recv, 4, slice(0, TILE))
    grad_features[...] = (spread[...].astype(F32) + total).astype(BF)
    ends = sum_ref(recv, 4, slice(TILE, TILE + TAIL))
    part = ends[0:PIECE].astype(BF)
    for y in range(4):
        piece[y] = part
    grad_bias[...] = (ends[PIECE : PIECE + 1] + ends[PIECE + 1 : PIECE + 2]) * NORM


def exchange(value, axis):
    return lax.all_to_all(value, axis, 0, 0)


ALONG_X = [[[(x * 4 + z) * 2 + k for x in range(4)] for z in range(4)] for k in range(2)]
ALONG_Z = [[[(x * 4 + z) * 2 + k for z in range(4)] for x in range(4)] for k in range(2)]
FIRST = ALONG_X[0] + ALONG_Z[1]
SECOND = ALONG_Z[0] + ALONG_X[1]


def exchange_col(value, groups):
    return lax.all_to_all(value, COL, 0, 0, axis_index_groups=groups)


def along_y(*blocks):
    return [
        lax.ppermute(block, "y", [(i, (i + d) % 4) for i in range(4)])
        for d, block in enumerate(blocks, 1)
    ]


def copies(value):
    return jnp.broadcast_to(value[None], (4,) + value.shape)


def shards(features, grad_out, weight, bias, tile_rows, tile_cols, tile_weights, tile_count):
    shape = jax.ShapeDtypeStruct
    rows, cols = tile_rows[0], tile_cols[0]
    tiles = tile_weights[0, 0]
    core, zh, y = (lax.axis_index(a).astype(jnp.int32).reshape(1) for a in ("k", "zh", "y"))
    swap = [(0, 1), (1, 0)]

    own = exchange(copies(features), "zl")
    own = exchange(copies(own), "x").reshape(16, TILE, H)
    other = lax.ppermute(own, "k", swap)
    flags = (pltpu.SMEM((16,), jnp.int32), pltpu.SMEM((32,), jnp.int32))
    scratch = (pltpu.VMEM((16, TILE, H), F32),) + flags
    begun, mass = call(
        own_kernel,
        (shape((16, TILE, H), F32), shape((16, EXTRA, TILE), F32)),
        4,
        2,
        flags,
        300000000,
    )(rows, cols, tile_count, core, tiles, own)
    one_block = shape((TILE + EXTRA, H), BF)
    part, near1, near2, near3, mine = call(
        forward_kernel,
        (shape((4, 3, TILE + EXTRA, H), BF),) + (one_block,) * 4,
        6,
        4,
        (pltpu.VMEM((16, TILE, H), F32), pltpu.VMEM((16, EXTRA, TILE), F32)) + flags,
        300000000,
    )(rows, cols, tile_count, core, zh, y, tiles, other, begun, mass)
    part = exchange(part, "y")
    part = call(sum_y_kernel, shape((4, TILE + EXTRA, H), BF), 1, 1)(zh, part)
    part = exchange(part, "zh")
    near = along_y(near1, near2, near3)
    node_out, spread, send = call(
        node_kernel,
        (shape((TILE, H), BF), shape((TILE, H), BF), shape((4, 2 * TILE + EXTRA, H), BF)),
        0,
        9,
    )(part, mine, *near, features, grad_out, weight, bias.reshape(1, H))
    send = exchange(send, "zh")
    send, *near = lax.optimization_barrier([send, *along_y(spread, spread, spread)])
    send = call(four_kernel, shape((4, 3 * TILE + TAIL, H), BF), 1, 2)(zh, send, weight)
    send = exchange(send, "y")
    flat = shape((16 * TILE + TAIL, H), BF)
    def terms(flip):
        return call(
            functools.partial(backward_kernel, flip),
            flat,
            6,
            6,
            (pltpu.VMEM((4, TILE, H), BF),) + scratch,
            300000000,
        )(rows, cols, tile_count, core, zh, y, tiles, send, spread, *near)

    back = lax.ppermute(terms(1), "k", swap)
    keep = terms(0)
    back = call(sum_k_kernel, shape((4, 4 * TILE + TAIL, H), BF), 1, 2)(
        core, keep, back
    )
    back = exchange_col(back, FIRST)
    back = call(sum_x_kernel, shape((4, TILE + TAIL, H), BF), 0, 1)(back)
    back = exchange_col(back, SECOND)
    grad_features, piece, grad_bias = call(
        last_kernel, (shape((TILE, H), BF), shape((4, PIECE, H), BF), shape((1, H), F32)), 0, 2
    )(back, spread)
    grad_weight = exchange(piece, "y").reshape(H, H).astype(F32) * NORM
    return (node_out, grad_features, grad_weight, grad_bias.reshape(H))


def solution(mesh):
    grid = Mesh(mesh.devices.reshape(SIZES), AXES)
    nodes = P(COL + ROW, None)
    return jax.shard_map(
        shards,
        mesh=grid,
        in_specs=(
            nodes,
            nodes,
            P(),
            P(),
            P(COL, ROW, None),
            P(COL, ROW, None),
            P(COL, ROW, None, None, None),
            P(COL, ROW),
        ),
        out_specs=(nodes, nodes, P(), P()),
        check_vma=False,
    )
```

```python
import functools

import jax
import jax.numpy as jnp
from jax import lax
from jax.experimental import pallas as pl
from jax.experimental.pallas import tpu as pltpu
from jax.sharding import Mesh, PartitionSpec as P

AXES = ("x", "zl", "k", "zh", "y")
SIZES = (4, 4, 2, 4, 4)
COL, ROW = ("x", "zl", "k"), ("zh", "y")
TILE, H, EXTRA = 128, 256, 16
PIECE = H // 4
TAIL = PIECE + EXTRA
NORM = 1.0 / 256.0
BF, F32 = jnp.bfloat16, jnp.float32


def call(kernel, outs, in_smem, n_in, scratch=(), flops=1000000):
    vmem = pl.BlockSpec(memory_space=pltpu.VMEM)
    smem = pl.BlockSpec(memory_space=pltpu.SMEM)
    return pl.pallas_call(
        kernel,
        out_shape=outs,
        in_specs=[smem] * in_smem + [vmem] * n_in,
        out_specs=jax.tree.map(lambda _: vmem, outs),
        scratch_shapes=list(scratch),
        compiler_params=pltpu.CompilerParams(vmem_limit_bytes=40 * 1024 * 1024),
        cost_estimate=pl.CostEstimate(flops=flops, bytes_accessed=4000000, transcendentals=0),
    )


def split_rows(total):
    high = total.astype(BF).astype(F32)
    low = total - high
    row = lax.broadcasted_iota(jnp.int32, (EXTRA, H), 0)
    return jnp.where(row == 0, high, jnp.where(row == 1, low, 0.0)).astype(BF)


def sum_ref(ref, count, rows):
    total = ref[0, rows, :].astype(F32)
    for i in range(1, count):
        total += ref[i, rows, :].astype(F32)
    return total


def mass_rows(mass):
    high = mass.astype(BF)
    low = (mass - high.astype(F32)).astype(BF)
    return jnp.concatenate([high, low], axis=1)


def each_slot(count, step):
    def pair(i, carry):
        step(2 * i)
        step(2 * i + 1)
        return carry

    lax.fori_loop(0, count // 2, pair, 0)

    @pl.when(lax.rem(count, 2) == 1)
    def _():
        step(count - 1)


def clear(seen, count):
    for i in range(count):
        seen[i] = 0


def slots_of(cols, count, parity, order):
    def put(t, n):
        order[n] = t
        return n + jnp.where(lax.rem(cols[0, t], 2) == parity, 1, 0)

    return lax.fori_loop(0, count, put, 0)


def row_sums(ones, tile):
    return lax.dot_general(ones, tile, (((1,), (1,)), ((), ())), preferred_element_type=F32)


def own_kernel(rows, cols, count, core, tiles, own, begun, mass, seen, order):
    clear(seen, 16)
    mass[...] = jnp.zeros_like(mass)
    ones = jnp.ones((EXTRA, TILE), BF)

    def step(i):
        t = order[i]
        r = rows[0, t]
        tile = tiles[t]
        product = jnp.dot(tile, own[cols[0, t] // 2], preferred_element_type=F32)
        begun[r] = jnp.where(seen[r] == 1, begun[r], 0.0) + product
        mass[r] += row_sums(ones, tile)
        seen[r] = 1

    each_slot(slots_of(cols, count[0, 0], core[0], order), step)


def forward_kernel(
    rows, cols, count, core, zh, y, tiles, other, begun, masses, far, near1, near2, near3, mine, acc, mass, seen, order
):
    clear(seen, 16)
    mass[...] = masses[...]
    ones = jnp.ones((EXTRA, TILE), BF)

    def mark(i, carry):
        seen[rows[0, order[i]]] = 1
        return carry

    lax.fori_loop(0, slots_of(cols, count[0, 0], core[0], order), mark, 0)

    def so_far(r):
        return jnp.where(seen[r] == 2, acc[r], jnp.where(seen[r] == 1, begun[r], 0.0))

    def step(i):
        t = order[i]
        r = rows[0, t]
        tile = tiles[t]
        acc[r] = so_far(r) + jnp.dot(tile, other[cols[0, t] // 2], preferred_element_type=F32)
        mass[r] += row_sums(ones, tile)
        seen[r] = 2

    each_slot(slots_of(cols, count[0, 0], 1 - core[0], order), step)

    for to in range(4):
        blocks = [4 * lax.rem(zh[0] + d, 4) + to for d in (1, 2, 3)]
        for d, r in enumerate(blocks):
            far[to, d * TILE : (d + 1) * TILE, :] = so_far(r).astype(BF)
        one, two, three = (mass[r] for r in blocks)
        row = lax.broadcasted_iota(jnp.int32, (EXTRA, TILE), 0)
        far[to, 3 * TILE :, :] = mass_rows(
            jnp.where(row == 0, one, jnp.where(row == 1, two, three))
        )
    for d, out in enumerate((mine, near1, near2, near3)):
        r = 4 * zh[0] + lax.rem(y[0] + d, 4)
        out[0:TILE, :] = so_far(r).astype(BF)
        out[TILE:, :] = mass_rows(mass[r])


def zh_rank(core, z):
    return jnp.where(core[0] == 0, z, 3 - z)


def sum_y_kernel(core, zh, recv, out):
    out[zh_rank(core, zh[0])] = jnp.zeros((TILE + EXTRA, H), BF)
    ends = sum_ref(recv, 4, slice(3 * TILE, 3 * TILE + EXTRA))
    masses = ends[:, 0:TILE] + ends[:, TILE:]
    for d in range(3):
        z = zh_rank(core, lax.rem(zh[0] + d + 1, 4))
        out[z, 0:TILE, :] = sum_ref(recv, 4, slice(d * TILE, (d + 1) * TILE)).astype(BF)
        out[z, TILE:, :] = mass_rows(jnp.broadcast_to(masses[d : d + 1], (EXTRA, TILE)))


def column(lanes):
    on_diagonal = lax.broadcasted_iota(jnp.int32, (TILE, TILE), 0) == lax.broadcasted_iota(
        jnp.int32, (TILE, TILE), 1
    )
    return jnp.sum(jnp.where(on_diagonal, lanes, 0.0), axis=1, keepdims=True)


def node_kernel(
    recv, mine, near1, near2, near3, features, grad_out, weight, bias, node_out, spread_out, send
):
    total = mine[...].astype(F32) + recv[0].astype(F32)
    for block in (recv[1], recv[2], recv[3], near1[...], near2[...], near3[...]):
        total += block.astype(F32)
    ends = total[TILE:]
    degrees = 1.0 + ends[:, 0:TILE] + ends[:, TILE:]
    degree = column(degrees[0:1])
    aggregate = ((features[...].astype(F32) + total[0:TILE]) / degree).astype(BF)
    w = weight[...]
    pre = jnp.dot(aggregate, w, preferred_element_type=F32) + bias[...]
    sig = jax.nn.sigmoid(pre)
    node_out[...] = (pre * sig).astype(BF)
    grad_pre = (grad_out[...].astype(F32) * (sig * (1.0 + pre * (1.0 - sig)))).astype(BF)
    back = lax.dot_general(grad_pre, w, (((1,), (1,)), ((), ())), preferred_element_type=F32)
    spread_out[...] = (back / degree).astype(BF)
    degree_rows = mass_rows(degrees)
    send[0:TILE, :] = grad_pre
    send[TILE : 2 * TILE, :] = aggregate
    send[2 * TILE :, :] = degree_rows


def four_kernel(recv, weight, out):
    w = weight[...]
    term = jnp.zeros((H, H), F32)
    bias_term = jnp.zeros((1, H), F32)
    for z in range(4):
        grad_pre = recv[z, 0:TILE, :]
        ends = recv[z, 2 * TILE :, :].astype(F32)
        degree = column(ends[0:1, 0:TILE] + ends[0:1, TILE:])
        back = lax.dot_general(grad_pre, w, (((1,), (1,)), ((), ())), preferred_element_type=F32)
        spread = (back / degree).astype(BF)
        for y in range(4):
            out[y, z * TILE : (z + 1) * TILE, :] = spread
        term += lax.dot_general(
            recv[z, TILE : 2 * TILE, :],
            grad_pre,
            (((0,), (0,)), ((), ())),
            preferred_element_type=F32,
        )
        bias_term += jnp.sum(grad_pre.astype(F32), axis=0, keepdims=True)
    bias_rows = split_rows(bias_term)
    for y in range(4):
        out[y, 4 * TILE : 4 * TILE + PIECE, :] = term[PIECE * y : PIECE * (y + 1)].astype(BF)
        out[y, 4 * TILE + PIECE :, :] = bias_rows


def tail_sum(total):
    ends = split_rows(total[PIECE : PIECE + 1] + total[PIECE + 1 : PIECE + 2])
    return jnp.concatenate([total[0:PIECE].astype(BF), ends], axis=0)


def backward_kernel(flip, rows, cols, count, core, tiles, spread, out, acc, seen, order):
    clear(seen, 16)
    parity = 1 - core[0] if flip else core[0]

    def step(i):
        t = order[i]
        c, r = cols[0, t] // 2, rows[0, t]
        start = pl.multiple_of((r // 4) * TILE, TILE)
        block = spread[lax.rem(r, 4), pl.ds(start, TILE), :]
        product = lax.dot_general(
            tiles[t], block, (((0,), (0,)), ((), ())), preferred_element_type=F32
        )
        acc[c] = jnp.where(seen[c] == 1, acc[c], 0.0) + product
        seen[c] = 1

    each_slot(slots_of(cols, count[0, 0], parity, order), step)
    for i in range(16):
        out[i * TILE : (i + 1) * TILE, :] = jnp.where(seen[i] == 1, acc[i], 0.0).astype(BF)
    out[16 * TILE :, :] = tail_sum(sum_ref(spread, 4, slice(4 * TILE, 4 * TILE + TAIL)))


def sum_k_kernel(core, keep, recv, out):
    def both(rows):
        return keep[rows, :].astype(F32) + recv[rows, :].astype(F32)

    tail = tail_sum(both(slice(16 * TILE, 16 * TILE + TAIL)))
    first = core[0] == 0
    for d in range(4):
        for e in range(4):
            i = jnp.where(first, 4 * d + e, 4 * e + d)
            rows = pl.ds(pl.multiple_of(i * TILE, TILE), TILE)
            out[d, e * TILE : (e + 1) * TILE, :] = both(rows).astype(BF)
        out[d, 4 * TILE :, :] = tail


def sum_x_kernel(recv, out):
    tail = tail_sum(sum_ref(recv, 4, slice(4 * TILE, 4 * TILE + TAIL)))
    for z in range(4):
        out[z, 0:TILE, :] = sum_ref(recv, 4, slice(z * TILE, (z + 1) * TILE)).astype(BF)
        out[z, TILE:, :] = tail


def last_kernel(recv, spread, grad_features, piece, grad_bias):
    total = sum_ref(recv, 4, slice(0, TILE))
    grad_features[...] = (spread[...].astype(F32) + total).astype(BF)
    ends = sum_ref(recv, 4, slice(TILE, TILE + TAIL))
    part = ends[0:PIECE].astype(BF)
    for y in range(4):
        piece[y] = part
    grad_bias[...] = (ends[PIECE : PIECE + 1] + ends[PIECE + 1 : PIECE + 2]) * NORM


def exchange(value, axis):
    return lax.all_to_all(value, axis, 0, 0)


ALONG_X = [[[(x * 4 + z) * 2 + k for x in range(4)] for z in range(4)] for k in range(2)]
ALONG_Z = [[[(x * 4 + z) * 2 + k for z in range(4)] for x in range(4)] for k in range(2)]
FIRST = ALONG_X[0] + ALONG_Z[1]
SECOND = ALONG_Z[0] + ALONG_X[1]


def exchange_col(value, groups):
    return lax.all_to_all(value, COL, 0, 0, axis_index_groups=groups)


def exchange_zh(value):
    groups = [[0, 1, 2, 3], [7, 6, 5, 4]]
    return lax.all_to_all(value, ("k", "zh"), 0, 0, axis_index_groups=groups)


def along_y(*blocks):
    return [
        lax.ppermute(block, "y", [(i, (i + d) % 4) for i in range(4)])
        for d, block in enumerate(blocks, 1)
    ]


def copies(value):
    return jnp.broadcast_to(value[None], (4,) + value.shape)


def shards(features, grad_out, weight, bias, tile_rows, tile_cols, tile_weights, tile_count):
    shape = jax.ShapeDtypeStruct
    rows, cols = tile_rows[0], tile_cols[0]
    tiles = tile_weights[0, 0]
    core, zh, y = (lax.axis_index(a).astype(jnp.int32).reshape(1) for a in ("k", "zh", "y"))
    swap = [(0, 1), (1, 0)]

    own = exchange(copies(features), "zl")
    own = exchange(copies(own), "x").reshape(16, TILE, H)
    other = lax.ppermute(own, "k", swap)
    flags = (pltpu.SMEM((16,), jnp.int32), pltpu.SMEM((32,), jnp.int32))
    scratch = (pltpu.VMEM((16, TILE, H), F32),) + flags
    begun, mass = call(
        own_kernel,
        (shape((16, TILE, H), F32), shape((16, EXTRA, TILE), F32)),
        4,
        2,
        flags,
        300000000,
    )(rows, cols, tile_count, core, tiles, own)
    one_block = shape((TILE + EXTRA, H), BF)
    part, near1, near2, near3, mine = call(
        forward_kernel,
        (shape((4, 3 * TILE + EXTRA, H), BF),) + (one_block,) * 4,
        6,
        4,
        (pltpu.VMEM((16, TILE, H), F32), pltpu.VMEM((16, EXTRA, TILE), F32)) + flags,
        300000000,
    )(rows, cols, tile_count, core, zh, y, tiles, other, begun, mass)
    part = exchange(part, "y")
    part = call(sum_y_kernel, shape((4, TILE + EXTRA, H), BF), 2, 1)(core, zh, part)
    part = exchange_zh(part)
    near = along_y(near1, near2, near3)
    node_out, spread, send = call(
        node_kernel,
        (shape((TILE, H), BF), shape((TILE, H), BF), shape((2 * TILE + EXTRA, H), BF)),
        0,
        9,
    )(part, mine, *near, features, grad_out, weight, bias.reshape(1, H))
    send = lax.all_gather(send, "zh")
    send = call(four_kernel, shape((4, 4 * TILE + TAIL, H), BF), 0, 2)(send, weight)
    send = exchange(send, "y")
    flat = shape((16 * TILE + TAIL, H), BF)
    def terms(flip):
        return call(
            functools.partial(backward_kernel, flip),
            flat,
            4,
            2,
            scratch,
            300000000,
        )(rows, cols, tile_count, core, tiles, send)

    back = lax.ppermute(terms(1), "k", swap)
    keep = terms(0)
    back = call(sum_k_kernel, shape((4, 4 * TILE + TAIL, H), BF), 1, 2)(
        core, keep, back
    )
    back = exchange_col(back, FIRST)
    back = call(sum_x_kernel, shape((4, TILE + TAIL, H), BF), 0, 1)(back)
    back = exchange_col(back, SECOND)
    grad_features, piece, grad_bias = call(
        last_kernel, (shape((TILE, H), BF), shape((4, PIECE, H), BF), shape((1, H), F32)), 0, 2
    )(back, spread)
    grad_weight = exchange(piece, "y").reshape(H, H).astype(F32) * NORM
    return (node_out, grad_features, grad_weight, grad_bias.reshape(H))


def solution(mesh):
    grid = Mesh(mesh.devices.reshape(SIZES), AXES)
    nodes = P(COL + ROW, None)
    return jax.shard_map(
        shards,
        mesh=grid,
        in_specs=(
            nodes,
            nodes,
            P(),
            P(),
            P(COL, ROW, None),
            P(COL, ROW, None),
            P(COL, ROW, None, None, None),
            P(COL, ROW),
        ),
        out_specs=(nodes, nodes, P(), P()),
        check_vma=False,
    )
```

```python
import functools

import jax
import jax.numpy as jnp
from jax import lax
from jax.experimental import pallas as pl
from jax.experimental.pallas import tpu as pltpu
from jax.sharding import Mesh, PartitionSpec as P

AXES = ("x", "zl", "k", "zh", "y")
SIZES = (4, 4, 2, 4, 4)
COL, ROW = ("x", "zl", "k"), ("zh", "y")
TILE, H, EXTRA = 128, 256, 16
PIECE = H // 4
TAIL = PIECE + EXTRA
NORM = 1.0 / 256.0
BF, F32 = jnp.bfloat16, jnp.float32


def call(kernel, outs, in_smem, n_in, scratch=(), flops=1000000):
    vmem = pl.BlockSpec(memory_space=pltpu.VMEM)
    smem = pl.BlockSpec(memory_space=pltpu.SMEM)
    return pl.pallas_call(
        kernel,
        out_shape=outs,
        in_specs=[smem] * in_smem + [vmem] * n_in,
        out_specs=jax.tree.map(lambda _: vmem, outs),
        scratch_shapes=list(scratch),
        compiler_params=pltpu.CompilerParams(vmem_limit_bytes=40 * 1024 * 1024),
        cost_estimate=pl.CostEstimate(flops=flops, bytes_accessed=4000000, transcendentals=0),
    )


def split_rows(total):
    high = total.astype(BF).astype(F32)
    low = total - high
    row = lax.broadcasted_iota(jnp.int32, (EXTRA, H), 0)
    return jnp.where(row == 0, high, jnp.where(row == 1, low, 0.0)).astype(BF)


def sum_ref(ref, count, rows):
    total = ref[0, rows, :].astype(F32)
    for i in range(1, count):
        total += ref[i, rows, :].astype(F32)
    return total


def mass_rows(mass):
    high = mass.astype(BF)
    low = (mass - high.astype(F32)).astype(BF)
    return jnp.concatenate([high, low], axis=1)


def each_slot(count, step):
    def pair(i, carry):
        step(2 * i)
        step(2 * i + 1)
        return carry

    lax.fori_loop(0, count // 2, pair, 0)

    @pl.when(lax.rem(count, 2) == 1)
    def _():
        step(count - 1)


def clear(seen, count):
    for i in range(count):
        seen[i] = 0


def slots_of(cols, count, parity, order):
    def put(t, n):
        order[n] = t
        return n + jnp.where(lax.rem(cols[0, t], 2) == parity, 1, 0)

    return lax.fori_loop(0, count, put, 0)


def row_sums(ones, tile):
    return lax.dot_general(ones, tile, (((1,), (1,)), ((), ())), preferred_element_type=F32)


def own_kernel(rows, cols, count, core, tiles, own, begun, mass, seen, order):
    clear(seen, 16)
    mass[...] = jnp.zeros_like(mass)
    ones = jnp.ones((EXTRA, TILE), BF)

    def step(i):
        t = order[i]
        r = rows[0, t]
        tile = tiles[t]
        product = jnp.dot(tile, own[cols[0, t] // 2], preferred_element_type=F32)
        begun[r] = jnp.where(seen[r] == 1, begun[r], 0.0) + product
        mass[r] += row_sums(ones, tile)
        seen[r] = 1

    each_slot(slots_of(cols, count[0, 0], core[0], order), step)


def forward_kernel(
    rows, cols, count, core, zh, y, tiles, other, begun, masses, far, near1, near2, near3, mine, acc, mass, seen, order
):
    clear(seen, 16)
    mass[...] = masses[...]
    ones = jnp.ones((EXTRA, TILE), BF)

    def mark(i, carry):
        seen[rows[0, order[i]]] = 1
        return carry

    lax.fori_loop(0, slots_of(cols, count[0, 0], core[0], order), mark, 0)

    def so_far(r):
        return jnp.where(seen[r] == 2, acc[r], jnp.where(seen[r] == 1, begun[r], 0.0))

    def step(i):
        t = order[i]
        r = rows[0, t]
        tile = tiles[t]
        acc[r] = so_far(r) + jnp.dot(tile, other[cols[0, t] // 2], preferred_element_type=F32)
        mass[r] += row_sums(ones, tile)
        seen[r] = 2

    each_slot(slots_of(cols, count[0, 0], 1 - core[0], order), step)

    for to in range(4):
        blocks = [4 * lax.rem(zh[0] + d, 4) + to for d in (1, 2, 3)]
        for d, r in enumerate(blocks):
            far[to, d * TILE : (d + 1) * TILE, :] = so_far(r).astype(BF)
        row = lax.broadcasted_iota(jnp.int32, (EXTRA, TILE), 0)
        masses = mass[to]
        for z in (1, 2, 3):
            masses = jnp.where(row == z, mass[4 * z + to], masses)
        far[to, 3 * TILE :, :] = mass_rows(masses)
    for d, out in enumerate((mine, near1, near2, near3)):
        out[...] = so_far(4 * zh[0] + lax.rem(y[0] + d, 4)).astype(BF)


def zh_rank(core, z):
    return jnp.where(core[0] == 0, z, 3 - z)


def sum_y_kernel(core, zh, recv, out):
    ends = sum_ref(recv, 4, slice(3 * TILE, 3 * TILE + EXTRA))
    masses = mass_rows(ends[:, 0:TILE] + ends[:, TILE:])
    for z in range(4):
        out[z, TILE:, :] = masses
    out[zh_rank(core, zh[0]), 0:TILE, :] = jnp.zeros((TILE, H), BF)
    for d in range(3):
        z = zh_rank(core, lax.rem(zh[0] + d + 1, 4))
        out[z, 0:TILE, :] = sum_ref(recv, 4, slice(d * TILE, (d + 1) * TILE)).astype(BF)


def column(lanes):
    on_diagonal = lax.broadcasted_iota(jnp.int32, (TILE, TILE), 0) == lax.broadcasted_iota(
        jnp.int32, (TILE, TILE), 1
    )
    return jnp.sum(jnp.where(on_diagonal, lanes, 0.0), axis=1, keepdims=True)


def node_kernel(
    zh, recv, mine, near1, near2, near3, features, grad_out, weight, bias, node_out, spread_out, send, degrees
):
    parts = [recv[z, 0:TILE, :] for z in range(4)] + [near1[...], near2[...], near3[...]]
    total = mine[...].astype(F32)
    for block in parts:
        total += block.astype(F32)
    ends = sum_ref(recv, 4, slice(TILE, TILE + EXTRA))
    rows = 1.0 + ends[:, 0:TILE] + ends[:, TILE:]
    degrees[...] = rows
    here = lax.broadcasted_iota(jnp.int32, (EXTRA, TILE), 0) == zh[0]
    degree = column(jnp.sum(jnp.where(here, rows, 0.0), axis=0, keepdims=True))
    aggregate = ((features[...].astype(F32) + total[0:TILE]) / degree).astype(BF)
    w = weight[...]
    pre = jnp.dot(aggregate, w, preferred_element_type=F32) + bias[...]
    sig = jax.nn.sigmoid(pre)
    node_out[...] = (pre * sig).astype(BF)
    grad_pre = (grad_out[...].astype(F32) * (sig * (1.0 + pre * (1.0 - sig)))).astype(BF)
    back = lax.dot_general(grad_pre, w, (((1,), (1,)), ((), ())), preferred_element_type=F32)
    spread_out[...] = (back / degree).astype(BF)
    send[0:TILE, :] = grad_pre
    send[TILE : 2 * TILE, :] = aggregate


def four_kernel(recv, degrees, weight, out):
    w = weight[...]
    term = jnp.zeros((H, H), F32)
    bias_term = jnp.zeros((1, H), F32)
    for z in range(4):
        grad_pre = recv[z, 0:TILE, :]
        degree = column(degrees[z : z + 1, :])
        back = lax.dot_general(grad_pre, w, (((1,), (1,)), ((), ())), preferred_element_type=F32)
        spread = (back / degree).astype(BF)
        for y in range(4):
            out[y, z * TILE : (z + 1) * TILE, :] = spread
        term += lax.dot_general(
            recv[z, TILE : 2 * TILE, :],
            grad_pre,
            (((0,), (0,)), ((), ())),
            preferred_element_type=F32,
        )
        bias_term += jnp.sum(grad_pre.astype(F32), axis=0, keepdims=True)
    bias_rows = split_rows(bias_term)
    for y in range(4):
        out[y, 4 * TILE : 4 * TILE + PIECE, :] = term[PIECE * y : PIECE * (y + 1)].astype(BF)
        out[y, 4 * TILE + PIECE :, :] = bias_rows


def tail_sum(total):
    ends = split_rows(total[PIECE : PIECE + 1] + total[PIECE + 1 : PIECE + 2])
    return jnp.concatenate([total[0:PIECE].astype(BF), ends], axis=0)


def backward_kernel(flip, rows, cols, count, core, tiles, spread, out, acc, seen, order):
    clear(seen, 16)
    parity = 1 - core[0] if flip else core[0]

    def step(i):
        t = order[i]
        c, r = cols[0, t] // 2, rows[0, t]
        start = pl.multiple_of((r // 4) * TILE, TILE)
        block = spread[lax.rem(r, 4), pl.ds(start, TILE), :]
        product = lax.dot_general(
            tiles[t], block, (((0,), (0,)), ((), ())), preferred_element_type=F32
        )
        acc[c] = jnp.where(seen[c] == 1, acc[c], 0.0) + product
        seen[c] = 1

    each_slot(slots_of(cols, count[0, 0], parity, order), step)
    for i in range(16):
        out[i * TILE : (i + 1) * TILE, :] = jnp.where(seen[i] == 1, acc[i], 0.0).astype(BF)
    out[16 * TILE :, :] = tail_sum(sum_ref(spread, 4, slice(4 * TILE, 4 * TILE + TAIL)))


def sum_k_kernel(core, keep, recv, out):
    def both(rows):
        return keep[rows, :].astype(F32) + recv[rows, :].astype(F32)

    tail = tail_sum(both(slice(16 * TILE, 16 * TILE + TAIL)))
    first = core[0] == 0
    for d in range(4):
        for e in range(4):
            i = jnp.where(first, 4 * d + e, 4 * e + d)
            rows = pl.ds(pl.multiple_of(i * TILE, TILE), TILE)
            out[d, e * TILE : (e + 1) * TILE, :] = both(rows).astype(BF)
        out[d, 4 * TILE :, :] = tail


def sum_x_kernel(recv, out):
    tail = tail_sum(sum_ref(recv, 4, slice(4 * TILE, 4 * TILE + TAIL)))
    for z in range(4):
        out[z, 0:TILE, :] = sum_ref(recv, 4, slice(z * TILE, (z + 1) * TILE)).astype(BF)
        out[z, TILE:, :] = tail


def last_kernel(recv, spread, grad_features, piece, grad_bias):
    total = sum_ref(recv, 4, slice(0, TILE))
    grad_features[...] = (spread[...].astype(F32) + total).astype(BF)
    ends = sum_ref(recv, 4, slice(TILE, TILE + TAIL))
    part = ends[0:PIECE].astype(BF)
    for y in range(4):
        piece[y] = part
    grad_bias[...] = (ends[PIECE : PIECE + 1] + ends[PIECE + 1 : PIECE + 2]) * NORM


def exchange(value, axis):
    return lax.all_to_all(value, axis, 0, 0)


ALONG_X = [[[(x * 4 + z) * 2 + k for x in range(4)] for z in range(4)] for k in range(2)]
ALONG_Z = [[[(x * 4 + z) * 2 + k for z in range(4)] for x in range(4)] for k in range(2)]
FIRST = ALONG_X[0] + ALONG_Z[1]
SECOND = ALONG_Z[0] + ALONG_X[1]


def exchange_col(value, groups):
    return lax.all_to_all(value, COL, 0, 0, axis_index_groups=groups)


def exchange_zh(value):
    groups = [[0, 1, 2, 3], [7, 6, 5, 4]]
    return lax.all_to_all(value, ("k", "zh"), 0, 0, axis_index_groups=groups)


def along_y(*blocks):
    return [
        lax.ppermute(block, "y", [(i, (i + d) % 4) for i in range(4)])
        for d, block in enumerate(blocks, 1)
    ]


def copies(value):
    return jnp.broadcast_to(value[None], (4,) + value.shape)


def shards(features, grad_out, weight, bias, tile_rows, tile_cols, tile_weights, tile_count):
    shape = jax.ShapeDtypeStruct
    rows, cols = tile_rows[0], tile_cols[0]
    tiles = tile_weights[0, 0]
    core, zh, y = (lax.axis_index(a).astype(jnp.int32).reshape(1) for a in ("k", "zh", "y"))
    swap = [(0, 1), (1, 0)]

    own = exchange(copies(features), "zl")
    own = exchange(copies(own), "x").reshape(16, TILE, H)
    other = lax.ppermute(own, "k", swap)
    flags = (pltpu.SMEM((16,), jnp.int32), pltpu.SMEM((32,), jnp.int32))
    scratch = (pltpu.VMEM((16, TILE, H), F32),) + flags
    begun, mass = call(
        own_kernel,
        (shape((16, TILE, H), F32), shape((16, EXTRA, TILE), F32)),
        4,
        2,
        flags,
        300000000,
    )(rows, cols, tile_count, core, tiles, own)
    one_block = shape((TILE, H), BF)
    part, near1, near2, near3, mine = call(
        forward_kernel,
        (shape((4, 3 * TILE + EXTRA, H), BF),) + (one_block,) * 4,
        6,
        4,
        (pltpu.VMEM((16, TILE, H), F32), pltpu.VMEM((16, EXTRA, TILE), F32)) + flags,
        300000000,
    )(rows, cols, tile_count, core, zh, y, tiles, other, begun, mass)
    part = exchange(part, "y")
    part = call(sum_y_kernel, shape((4, TILE + EXTRA, H), BF), 2, 1)(core, zh, part)
    part = exchange_zh(part)
    near = along_y(near1, near2, near3)
    node_out, spread, send, degrees = call(
        node_kernel,
        (
            shape((TILE, H), BF),
            shape((TILE, H), BF),
            shape((2 * TILE, H), BF),
            shape((EXTRA, TILE), F32),
        ),
        1,
        9,
    )(zh, part, mine, *near, features, grad_out, weight, bias.reshape(1, H))
    send = lax.all_gather(send, "zh")
    send = call(four_kernel, shape((4, 4 * TILE + TAIL, H), BF), 0, 3)(
        send, degrees, weight
    )
    send = exchange(send, "y")
    flat = shape((16 * TILE + TAIL, H), BF)
    def terms(flip):
        return call(
            functools.partial(backward_kernel, flip),
            flat,
            4,
            2,
            scratch,
            300000000,
        )(rows, cols, tile_count, core, tiles, send)

    back = lax.ppermute(terms(1), "k", swap)
    keep = terms(0)
    back = call(sum_k_kernel, shape((4, 4 * TILE + TAIL, H), BF), 1, 2)(
        core, keep, back
    )
    back = exchange_col(back, FIRST)
    back = call(sum_x_kernel, shape((4, TILE + TAIL, H), BF), 0, 1)(back)
    back = exchange_col(back, SECOND)
    grad_features, piece, grad_bias = call(
        last_kernel, (shape((TILE, H), BF), shape((4, PIECE, H), BF), shape((1, H), F32)), 0, 2
    )(back, spread)
    grad_weight = exchange(piece, "y").reshape(H, H).astype(F32) * NORM
    return (node_out, grad_features, grad_weight, grad_bias.reshape(H))


def solution(mesh):
    grid = Mesh(mesh.devices.reshape(SIZES), AXES)
    nodes = P(COL + ROW, None)
    return jax.shard_map(
        shards,
        mesh=grid,
        in_specs=(
            nodes,
            nodes,
            P(),
            P(),
            P(COL, ROW, None),
            P(COL, ROW, None),
            P(COL, ROW, None, None, None),
            P(COL, ROW),
        ),
        out_specs=(nodes, nodes, P(), P()),
        check_vma=False,
    )
```
